512 devices in a mesh: row: 16 (over x, y_lo, core), chan: 32 (over z, y_hi).
Axes of the slice: x: 4, y: 4 (y_hi: 2, y_lo: 2; y = y_hi * 2 + y_lo), z: 16, core: 2. Of those that a mesh axis runs over, the one named last changes fastest.
Arguments:
- pair: bfloat16 [1280, 1280, 128], P('row', 'chan'), may hold values from -6 to 6
- w_left_gate: bfloat16 [128, 128], replicated, may hold values from -0.5 to 0.5
- w_left: bfloat16 [128, 128], replicated, may hold values from -0.5 to 0.5
- w_right_gate: bfloat16 [128, 128], replicated, may hold values from -0.5 to 0.5
- w_right: bfloat16 [128, 128], replicated, may hold values from -0.5 to 0.5
- w_out_gate: bfloat16 [128, 128], replicated, may hold values from -0.5 to 0.5
- w_out: bfloat16 [128, 128], replicated, may hold values from -0.5 to 0.5
Outputs:
- update: bfloat16 [1280, 1280, 128], P('row', 'chan')
The draws below stay inside these ranges and needn't reach their ends.
All inputs are finite; a program needn't handle non-finite values.
Results may differ from the reference program's by a relative error of at most 0.0083.
Values may be sent and summed in bfloat16 or wider, within the bound.
A program may use at most 64 MiB of HBM per device.

```python
import jax
import jax.numpy as jnp
from jax import lax

C = 128
H = 128
ROW_DEV = 80
TOKENS = 1280
N_ROW = 16


def block_levels(key, extent, pieces, least, largest):
    def one(position, blocks):
        steps = jax.random.uniform(jax.random.fold_in(jax.random.fold_in(key, 6), position), (blocks,), jnp.float32, least / len(pieces), largest / len(pieces))
        return jnp.repeat(jnp.exp(steps), extent[position] // blocks).reshape((-1,) + (1,) * (len(extent) - position - 1))

    loudness = one(*pieces[0])
    for cut in pieces[1:]:
        loudness = loudness * one(*cut)
    return loudness


def normal_values(stream_key, dims, width, reach, shards=(), held_as=jnp.bfloat16):
    gain = block_levels(stream_key, dims, shards, -0.22, 0.18) if shards else 1.0
    values = jax.random.normal(stream_key, dims, jnp.float32) * width * gain
    return jnp.minimum(jnp.maximum(values, -reach), reach).astype(held_as)


def setup_inputs(seed: int = 0) -> dict:
    keys = jax.random.split(jax.random.key(seed), 8)
    return {
        "pair": normal_values(keys[0], (TOKENS, TOKENS, C), 1.0, 6.0, ((0, 16), (1, 32))),
        "w_left_gate": normal_values(keys[1], (C, H), C ** -0.5, 0.5),
        "w_left": normal_values(keys[2], (C, H), C ** -0.5, 0.5),
        "w_right_gate": normal_values(keys[3], (C, H), C ** -0.5, 0.5),
        "w_right": normal_values(keys[4], (C, H), C ** -0.5, 0.5),
        "w_out_gate": normal_values(keys[5], (C, C), C ** -0.5, 0.5),
        "w_out": normal_values(keys[6], (H, C), H ** -0.5, 0.5),
    }


def layer_norm(values, axis):
    mean = lax.optimization_barrier(jnp.mean(values, axis=axis, keepdims=True))
    centered = values - mean
    variance = lax.optimization_barrier(jnp.mean(centered * centered, axis=axis, keepdims=True))
    return centered * lax.rsqrt(variance + 1e-05)

def reference(pair, w_left_gate, w_left, w_right_gate, w_right, w_out_gate, w_out):
    normed = layer_norm(pair.astype(jnp.float32), -1).astype(jnp.bfloat16)
    flat = normed.reshape(TOKENS * TOKENS, C)

    def factor(weight_gate, weight_proj):
        gate_value = jnp.dot(flat, weight_gate, preferred_element_type=jnp.float32)
        proj_value = jnp.dot(flat, weight_proj, preferred_element_type=jnp.float32)
        return (jax.nn.sigmoid(gate_value) * proj_value).astype(jnp.bfloat16).reshape(TOKENS, TOKENS, H)
    left = factor(w_left_gate, w_left)
    right = factor(w_right_gate, w_right)
    right_wide = jnp.transpose(right, (2, 0, 1)).astype(jnp.float32)
    out_weight = w_out.astype(jnp.float32)
    gate_weight = w_out_gate.astype(jnp.float32)

    def one_block(first_row):
        left_block = lax.dynamic_slice_in_dim(left, first_row, ROW_DEV, 0).astype(jnp.float32)
        combined = jnp.einsum('ikh,hjk->hij', left_block, right_wide).astype(jnp.bfloat16)
        combined_normed = layer_norm(combined.astype(jnp.float32), 0).astype(jnp.bfloat16)
        linear = jnp.einsum('hij,hc->ijc', combined_normed.astype(jnp.float32), out_weight)
        normed_block = lax.dynamic_slice_in_dim(normed, first_row, ROW_DEV, 0).astype(jnp.float32)
        gate = jax.nn.sigmoid(jnp.einsum('ijc,cd->ijd', normed_block, gate_weight))
        return (gate * linear).astype(jnp.bfloat16)
    starts = (jnp.arange(N_ROW) * ROW_DEV).astype(jnp.int32)
    blocks = lax.map(one_block, starts)
    return blocks.reshape(TOKENS, TOKENS, C)
```

```python
import functools

import jax
import jax.numpy as jnp
from jax import lax
from jax.experimental import pallas as pl
from jax.experimental.pallas import tpu as pltpu
from jax.sharding import PartitionSpec as P

MESH = pl.DeviceIdType.MESH
F32, BF16 = jnp.float32, jnp.bfloat16
EPS = 1e-05
ROWS, COLS, CH = 80, 40, 128
PLANES, CHUNKS, STEP = 16, 5, 8
WIDE = STEP * ROWS
SHORT, SHORT_PAD = WIDE // 2, 384


def nt(a, b):
    return lax.dot_general(a, b, (((1,), (1,)), ((), ())), preferred_element_type=F32)


def tn(a, b):
    return lax.dot_general(a, b, (((0,), (0,)), ((), ())), preferred_element_type=F32)


def unfold(x, k):
    start = k * ROWS
    tile, off = start // 128, start % 128
    lo = x[:, tile * 128 : tile * 128 + 128]
    if off == 0:
        return lo
    lo = pltpu.roll(lo, 128 - off, 1)
    if off + ROWS <= 128:
        return lo
    hi = pltpu.roll(x[:, tile * 128 + 128 : tile * 128 + 256], 128 - off, 1)
    lane = lax.broadcasted_iota(jnp.int32, lo.shape, 1)
    return jnp.where(lane < 128 - off, lo, hi)


def fold(pieces):
    tiles = [None] * (-(-len(pieces) * ROWS // 128))
    lane = lax.broadcasted_iota(jnp.int32, pieces[0].shape, 1)
    for k, piece in enumerate(pieces):
        start = k * ROWS
        tile, off = start // 128, start % 128
        turned = pltpu.roll(piece, off, 1) if off else piece
        tiles[tile] = turned if tiles[tile] is None else jnp.where(lane < off, tiles[tile], turned)
        if off + ROWS > 128:
            tiles[tile + 1] = turned
    return jnp.concatenate(tiles, axis=1)


def kernel(
    pair_ref, wlg_ref, wl_ref, wrg_ref, wr_ref, wog_ref, wo_ref, out_ref,
    pair32, wt, ns, normed, gate, send, got, unf, tiles, left, right, acc, osend, oback, fbuf, fold_send, fold_got, lin,
    zs, zr, pls, prs, plr, prr, os_, or_, fs, fr,
):
    r, c = lax.axis_index("row"), lax.axis_index("chan")
    z, y = c // 2, lax.rem(c, 2)
    a, t, b = r // 8, lax.rem(r, 8), lax.rem(r, 2)
    h = (t // 2) * 2 + y
    half = pl.multiple_of(y * 128, 128)

    def owner(h_, a_, b_):
        return (a_ * 8 + (h_ // 2) * 2 + b_, z * 2 + lax.rem(h_, 2))

    def at_plane(z_):
        return (r, z_ * 2 + y)

    barrier = pltpu.get_barrier_semaphore()

    def greet_plane(d, carry):
        pl.semaphore_signal(barrier, inc=1, device_id=at_plane(lax.rem(z + d, PLANES)), device_id_type=MESH)
        return carry

    def greet_inside(d, carry):
        there = (lax.rem(r + d // 2, 16), z * 2 + lax.rem(y + lax.rem(d, 2), 2))
        pl.semaphore_signal(barrier, inc=1, device_id=there, device_id_type=MESH)
        return carry

    lax.fori_loop(1, PLANES, greet_plane, 0)
    lax.fori_loop(1, 32, greet_inside, 0)

    for n, ref in enumerate((wlg_ref, wl_ref, wrg_ref, wr_ref)):
        wt[n] = ref[...].astype(F32).T.astype(BF16)
    pair32[...] = pair_ref[...].astype(F32)

    def normalise(s):
        def eight_rows(g, carry):
            x = pair32[pl.ds(pl.multiple_of(g * 8, 8), 8), pl.ds(pl.multiple_of(s * STEP, STEP), STEP), :]
            centered = x - jnp.mean(x, axis=-1, keepdims=True)
            variance = jnp.mean(centered * centered, axis=-1, keepdims=True)
            at = pl.multiple_of(lax.rem(g, 5) * 16 + (g // 5) * 8, 8)
            ns[:, pl.ds(at, 8), :] = jnp.swapaxes(centered * lax.rsqrt(variance + EPS), 0, 1)
            return carry

        lax.fori_loop(0, 10, eight_rows, 0)
        normed[s] = ns[...].reshape(WIDE, CH).astype(BF16)

    def factors(s):
        n = normed[s]
        lf = (jax.nn.sigmoid(nt(wt[0], n)) * nt(wt[1], n)).reshape(PLANES, 8, WIDE)
        rf = (jax.nn.sigmoid(nt(wt[2], n)) * nt(wt[3], n)).reshape(PLANES, 8, WIDE)
        send[s] = jnp.concatenate([lf, rf], axis=1).astype(BF16)

    def send_planes(s):
        pltpu.make_async_copy(send.at[s, z], got.at[s, z], zr.at[s]).start()

        def one(d, carry):
            there = lax.rem(z + d, PLANES)
            pltpu.make_async_remote_copy(
                src_ref=send.at[s, there], dst_ref=got.at[s, z], send_sem=zs.at[s], recv_sem=zr.at[s],
                device_id=at_plane(there), device_id_type=MESH,
            ).start()
            return carry

        lax.fori_loop(1, PLANES, one, 0)

    def unfold_chunk(s):
        def two_planes(m, carry):
            for e in range(2):
                x = got[s, 2 * m + e].astype(F32)
                for k in range(STEP):
                    unf[:, e * STEP + k, :] = unfold(x, k)
            tiles[s, :, pl.ds(pl.multiple_of(m * 16, 16), 16), :] = unf[...].astype(BF16)
            return carry

        lax.fori_loop(0, PLANES // 2, two_planes, 0)

    def send_inside(s):
        to_left = left.at[s, pl.ds(half, 128), pl.ds(pl.multiple_of(t * 128, 128), 128)]
        to_right = right.at[s, pl.ds(half, 128), pl.ds(pl.multiple_of((r // 2) * 128, 128), 128)]
        for e in range(2):

            def one(d, carry, e=e):
                there = lax.rem(h + d, 8)
                pltpu.make_async_remote_copy(
                    src_ref=tiles.at[s, there], dst_ref=to_left, send_sem=pls.at[s], recv_sem=plr.at[s],
                    device_id=owner(there, a, lax.rem(b + e, 2)), device_id_type=MESH,
                ).start()
                pltpu.make_async_remote_copy(
                    src_ref=tiles.at[s, 8 + there], dst_ref=to_right, send_sem=prs.at[s], recv_sem=prr.at[s],
                    device_id=owner(there, lax.rem(a + e, 2), b), device_id_type=MESH,
                ).start()
                return carry

            lax.fori_loop(1 - e, 8, one, 0)
        pltpu.make_async_copy(tiles.at[s, h], to_left, plr.at[s]).start()
        pltpu.make_async_copy(tiles.at[s, 8 + h], to_right, prr.at[s]).start()

    def multiply(s, first):
        pltpu.make_async_copy(left.at[s], left.at[s], plr.at[s]).wait()
        pltpu.make_async_copy(right.at[s], right.at[s], prr.at[s]).wait()

        def one(m, carry):
            cols = right[s, :, pl.ds(pl.multiple_of(m * 128, 128), 128)]
            part = tn(cols, left[s])[:ROWS]
            acc[m] = part if first else acc[m] + part
            return carry

        lax.fori_loop(0, 8, one, 0)

    def send_back(q):
        for y_ in range(2):
            at = pl.multiple_of(q * 16, 16)
            rows = acc[:, pl.ds(at, 16), :][:, y_ * 8 : y_ * 8 + 8, :].reshape(64, 1024).astype(BF16)
            for t_ in range(8):
                osend[q, y_ * 8 + t_] = rows[:, t_ * 128 : t_ * 128 + 128]

        def one(d, carry):
            t_, y_ = lax.rem(t + d // 2, 8), lax.rem(y + lax.rem(d, 2), 2)
            pltpu.make_async_remote_copy(
                src_ref=osend.at[q, y_ * 8 + t_], dst_ref=oback.at[q, h, b], send_sem=os_.at[q], recv_sem=or_.at[q],
                device_id=(a * 8 + t_, z * 2 + y_), device_id_type=MESH,
            ).start()
            return carry

        lax.fori_loop(1, 16, one, 0)
        pltpu.make_async_copy(osend.at[q, y * 8 + t], oback.at[q, h, b], or_.at[q]).start()

    def view(buffer, g, plane):
        return buffer.at[g, plane] if g < 2 else buffer.at[g, plane, :, pl.ds(0, SHORT_PAD)]

    def fold_chunks(g):
        for q in (2 * g, 2 * g + 1) if g < 2 else (4,):
            pltpu.make_async_copy(oback.at[q], oback.at[q], or_.at[q]).wait()

        def pieces(q, b_, m2, e):
            fbuf[...] = oback[q, :, b_, pl.ds(pl.multiple_of(m2 * 16, 16), 16), :].astype(F32)
            return [fbuf[:, e * STEP + k, :] for k in range(STEP)]

        def two_planes(n, carry):
            b_, m2 = n // 4, lax.rem(n, 4)
            for e in range(2):
                plane = (2 * m2 + e) * 2 + b_
                if g < 2:
                    rows = [fold(pieces(2 * g + f, b_, m2, e)) for f in range(2)]
                    fold_send[g, plane] = jnp.concatenate(rows, axis=0).astype(BF16)
                else:
                    whole = pieces(4, b_, m2, e)
                    rows = [fold(whole[:4]), fold(whole[4:])]
                    fold_send[g, plane, :, :SHORT_PAD] = jnp.concatenate(rows, axis=0).astype(BF16)
            return carry

        lax.fori_loop(0, 8, two_planes, 0)
        pltpu.make_async_copy(view(fold_send, g, z), view(fold_got, g, z), fr.at[g]).start()

        def one(d, carry):
            there = lax.rem(z + d, PLANES)
            pltpu.make_async_remote_copy(
                src_ref=view(fold_send, g, there), dst_ref=view(fold_got, g, z), send_sem=fs.at[g], recv_sem=fr.at[g],
                device_id=at_plane(there), device_id_type=MESH,
            ).start()
            return carry

        lax.fori_loop(1, PLANES, one, 0)

    def project(x):
        centered = x - jnp.mean(x, axis=0, keepdims=True)
        variance = jnp.mean(centered * centered, axis=0, keepdims=True)
        return tn((centered * lax.rsqrt(variance + EPS)).astype(BF16), wo_ref[...])

    def finish(g):
        arrived = fold_got.at[g] if g < 2 else fold_got.at[g, :, :, pl.ds(0, SHORT_PAD)]
        pltpu.make_async_copy(arrived, arrived, fr.at[g]).wait()
        if g < 2:
            x = fold_got[g].astype(F32)
            for f in range(2):
                part = project(x[:, f * 8 : f * 8 + 8, :].reshape(CH, WIDE))
                lin[f] = (part * gate[2 * g + f]).reshape(STEP, ROWS, CH)
        else:
            x = fold_got[g, :, :, :SHORT_PAD].astype(F32)
            for f in range(2):
                part = project(x[:, f * 8 : f * 8 + 8, :].reshape(CH, SHORT_PAD))[:SHORT]
                lin[0, f * 4 : f * 4 + 4] = (part * gate[4, f * SHORT : f * SHORT + SHORT]).reshape(4, ROWS, CH)

        def eight_rows(n, carry):
            at = pl.multiple_of(lax.rem(n, 5) * 16 + (n // 5) * 8, 8)
            rows = pl.ds(pl.multiple_of(n * 8, 8), 8)
            if g < 2:
                both = [jnp.swapaxes(lin[f, :, pl.ds(at, 8), :], 0, 1) for f in range(2)]
                out_ref[rows, g * 16 : g * 16 + 16, :] = jnp.concatenate(both, axis=1).astype(BF16)
            else:
                out_ref[rows, 32:40, :] = jnp.swapaxes(lin[0, :, pl.ds(at, 8), :], 0, 1).astype(BF16)
            return carry

        lax.fori_loop(0, 10, eight_rows, 0)

    for s in range(CHUNKS):
        normalise(s)
        factors(s)
        if s == 0:
            pl.semaphore_wait(barrier, 46)
        send_planes(s)

    def gates(s, carry):
        gate[s] = jax.nn.sigmoid(jnp.dot(normed[s], wog_ref[...], preferred_element_type=F32))
        return carry

    lax.fori_loop(0, CHUNKS, gates, 0)

    for s in range(CHUNKS):
        pltpu.make_async_copy(got.at[s], got.at[s], zr.at[s]).wait()
        unfold_chunk(s)
        send_inside(s)
        if s:
            multiply(s - 1, s == 1)
    multiply(CHUNKS - 1, False)
    for q in range(CHUNKS):
        send_back(q)
    for g in range(3):
        fold_chunks(g)
    for g in range(3):
        finish(g)

    for s in range(CHUNKS):
        sent = got.at[s, pl.ds(0, PLANES - 1)]
        pltpu.make_async_copy(sent, sent, zs.at[s]).wait()
        sent = tiles.at[s, pl.ds(0, 15)]
        pltpu.make_async_copy(sent, sent, pls.at[s]).wait()
        pltpu.make_async_copy(sent, sent, prs.at[s]).wait()
        sent = osend.at[s, pl.ds(0, 15)]
        pltpu.make_async_copy(sent, sent, os_.at[s]).wait()
    for g in range(3):
        sent = fold_got.at[g, pl.ds(0, PLANES - 1)] if g < 2 else fold_got.at[g, pl.ds(0, PLANES - 1), :, pl.ds(0, SHORT_PAD)]
        pltpu.make_async_copy(sent, sent, fs.at[g]).wait()


def on_device(*args):
    vmem = pltpu.VMEM
    return pl.pallas_call(
        kernel,
        out_shape=jax.ShapeDtypeStruct((ROWS, COLS, CH), BF16),
        in_specs=[pl.BlockSpec(memory_space=vmem)] * 7,
        out_specs=pl.BlockSpec(memory_space=vmem),
        scratch_shapes=[
            vmem((ROWS, COLS, CH), F32),
            vmem((4, CH, CH), BF16),
            vmem((STEP, ROWS, CH), F32),
            vmem((CHUNKS, WIDE, CH), BF16),
            vmem((CHUNKS, WIDE, CH), F32),
            vmem((CHUNKS, PLANES, 16, WIDE), BF16),
            vmem((CHUNKS, PLANES, 16, WIDE), BF16),
            vmem((16, 16, CH), F32),
            vmem((CHUNKS, 16, 128, 128), BF16),
            vmem((CHUNKS, 256, 1024), BF16),
            vmem((CHUNKS, 256, 1024), BF16),
            vmem((8, ROWS, 1024), F32),
            vmem((CHUNKS, 16, 64, 128), BF16),
            vmem((CHUNKS, 8, 2, 64, 128), BF16),
            vmem((8, 16, CH), F32),
            vmem((3, PLANES, 16, WIDE), BF16),
            vmem((3, PLANES, 16, WIDE), BF16),
            vmem((2, STEP, ROWS, CH), F32),
        ]
        + [pltpu.SemaphoreType.DMA((CHUNKS,))] * 8
        + [pltpu.SemaphoreType.DMA((3,))] * 2,
        compiler_params=pltpu.CompilerParams(collective_id=0, has_side_effects=True, vmem_limit_bytes=48 * 2**20),
        cost_estimate=pl.CostEstimate(flops=2_000_000_000, bytes_accessed=4_000_000, transcendentals=2_000_000),
    )(*args)


def solution(mesh):
    in_specs = (P("row", "chan", None), P(), P(), P(), P(), P(), P())
    return jax.shard_map(
        on_device, mesh=mesh, in_specs=in_specs, out_specs=P("row", "chan", None), check_vma=False
    )
```

```python
import functools

import jax
import jax.numpy as jnp
from jax import lax
from jax.experimental import pallas as pl
from jax.experimental.pallas import tpu as pltpu
from jax.sharding import PartitionSpec as P

MESH = pl.DeviceIdType.MESH
F32, BF16 = jnp.float32, jnp.bfloat16
EPS = 1e-05
ROWS, COLS, CH = 80, 40, 128
PLANES, CHUNKS, STEP = 16, 5, 8
WIDE = STEP * ROWS
SHORT, SHORT_PAD = WIDE // 2, 384
CUT, REST = 384, 256
MOVES = [(0, 0, WIDE), (1, 0, WIDE), (2, 0, WIDE), (3, 0, WIDE), (4, 0, CUT), (4, CUT, REST)]
BACK = (2 * CUT, 2 * REST + SHORT_PAD)


def nt(a, b):
    return lax.dot_general(a, b, (((1,), (1,)), ((), ())), preferred_element_type=F32)


def tn(a, b):
    return lax.dot_general(a, b, (((0,), (0,)), ((), ())), preferred_element_type=F32)


def unfold(x, k):
    start = k * ROWS
    tile, off = start // 128, start % 128
    lo = x[:, tile * 128 : tile * 128 + 128]
    if off == 0:
        return lo
    lo = pltpu.roll(lo, 128 - off, 1)
    if off + ROWS <= 128:
        return lo
    hi = pltpu.roll(x[:, tile * 128 + 128 : tile * 128 + 256], 128 - off, 1)
    lane = lax.broadcasted_iota(jnp.int32, lo.shape, 1)
    return jnp.where(lane < 128 - off, lo, hi)


def fold(pieces, first, last):
    tiles = {}
    lane = lax.broadcasted_iota(jnp.int32, pieces[0].shape, 1)
    for k, piece in enumerate(pieces):
        tile, off = k * ROWS // 128, k * ROWS % 128
        turned = pltpu.roll(piece, off, 1) if off else piece
        tiles[tile] = jnp.where(lane < off, tiles[tile], turned) if tile in tiles else turned
        if off + ROWS > 128:
            tiles[tile + 1] = turned
    return jnp.concatenate([tiles[tile] for tile in range(first, last)], axis=1)


def mix_halves(first, second):
    low = lax.broadcasted_iota(jnp.int32, first.shape, 1) < 4
    return jnp.where(low, first, pltpu.roll(second, 4, 1)), jnp.where(low, pltpu.roll(first, 4, 1), second)


def kernel(
    pair_hbm, wlg_hbm, wl_hbm, wrg_hbm, wr_hbm, wog_hbm, wo_hbm, out_ref,
    pair_ref, weights, pair32, wt, ns, normed, gate, send, got, flip, tiles, left, right, lk, rk, acc,
    osend, oback, flip4, fsend, fsend4, fgot, fgot4, lin,
    ins, zs, zr, pls, prs, plr, prr, os_, or_, fs, fr,
):
    r, c = lax.axis_index("row"), lax.axis_index("chan")
    z, y = c // 2, lax.rem(c, 2)
    a, t, core = r // 8, lax.rem(r, 8), lax.rem(r, 2)
    b = lax.rem(r // 4, 2)
    m = a * 4 + lax.rem(r, 4)
    h = lax.rem(r // 2, 2) * 2 + y

    def owner(g, h_, a_, b_):
        return ((2 * a_ + b_) * 4 + (h_ // 2) * 2 + g, z * 2 + lax.rem(h_, 2))

    def at_plane(z_):
        return (r, z_ * 2 + y)

    loads = [pltpu.make_async_copy(pair_hbm, pair_ref, ins.at[0])]
    for n, ref in enumerate((wlg_hbm, wl_hbm, wrg_hbm, wr_hbm, wog_hbm, wo_hbm)):
        loads.append(pltpu.make_async_copy(ref, weights.at[n], ins.at[n + 1]))
    for load in loads:
        load.start()

    barrier = pltpu.get_barrier_semaphore()

    def greet_plane(d, carry):
        pl.semaphore_signal(barrier, inc=1, device_id=at_plane(lax.rem(z + d, PLANES)), device_id_type=MESH)
        return carry

    def greet_side(d, carry):
        there = (a * 8 + lax.rem(t + d // 2, 8), z * 2 + lax.rem(y + lax.rem(d, 2), 2))
        pl.semaphore_signal(barrier, inc=1, device_id=there, device_id_type=MESH)
        return carry

    def greet_across(d, carry):
        there = ((2 * (1 - a) + b) * 4 + d // 2, z * 2 + lax.rem(d, 2))
        pl.semaphore_signal(barrier, inc=1, device_id=there, device_id_type=MESH)
        return carry

    lax.fori_loop(1, PLANES, greet_plane, 0)
    lax.fori_loop(1, 16, greet_side, 0)
    lax.fori_loop(0, 8, greet_across, 0)

    for load in loads:
        load.wait()
    for n in range(2):
        lt = weights[n].astype(F32).T.reshape(PLANES, 8, CH)
        rt = weights[n + 2].astype(F32).T.reshape(PLANES, 8, CH)
        wt[n] = jnp.concatenate(mix_halves(lt, rt), axis=1).reshape(256, CH).astype(BF16)
    pair32[...] = pair_ref[...].astype(F32)

    def normalise(s):
        def eight_rows(g, carry):
            x = pair32[pl.ds(pl.multiple_of(g * 8, 8), 8), pl.ds(pl.multiple_of(s * STEP, STEP), STEP), :]
            centered = x - jnp.mean(x, axis=-1, keepdims=True)
            variance = jnp.mean(centered * centered, axis=-1, keepdims=True)
            at = pl.multiple_of(lax.rem(g, 5) * 16 + (g // 5) * 8, 8)
            ns[:, pl.ds(at, 8), :] = jnp.swapaxes(centered * lax.rsqrt(variance + EPS), 0, 1)
            return carry

        lax.fori_loop(0, 10, eight_rows, 0)
        normed[s] = ns[...].reshape(WIDE, CH).astype(BF16)

    def factors(s, w):
        n = normed[s]
        rows = pl.ds(pl.multiple_of(w * 64, 64), 64)
        return (jax.nn.sigmoid(nt(wt[0, rows, :], n)) * nt(wt[1, rows, :], n)).reshape(4, 16, WIDE)

    def send_planes(v):
        s, lanes = MOVES[v][0], pl.ds(MOVES[v][1], MOVES[v][2])
        to = got.at[s, z, :, lanes]
        pltpu.make_async_copy(send.at[s, z, :, lanes], to, zr.at[v]).start()

        def one(d, carry):
            there = lax.rem(z + d, PLANES)
            pltpu.make_async_remote_copy(
                src_ref=send.at[s, there, :, lanes], dst_ref=to, send_sem=zs.at[v], recv_sem=zr.at[v],
                device_id=at_plane(there), device_id_type=MESH,
            ).start()
            return carry

        lax.fori_loop(1, PLANES, one, 0)

    def single(w, carry):
        send[0, pl.ds(w * 4, 4)] = factors(4, w).astype(BF16)
        return carry

    def double(p):
        def one(w, carry):
            v, u = factors(2 * p, w), factors(2 * p + 1, w)
            send[1 + p, pl.ds(w * 4, 4)] = jnp.concatenate([v[:, :8], u[:, :8]], axis=1).astype(BF16)
            send[3 + p, pl.ds(w * 4, 4)] = jnp.concatenate([v[:, 8:], u[:, 8:]], axis=1).astype(BF16)
            return carry

        lax.fori_loop(0, 4, one, 0)

    def arrive(v):
        arrived = got.at[MOVES[v][0], :, :, pl.ds(MOVES[v][1], MOVES[v][2])]
        pltpu.make_async_copy(arrived, arrived, zr.at[v]).wait()

    def turn(v):
        s, at, wide = MOVES[v]

        def one(z_, carry):
            flip[:, z_, at : at + wide] = got[s, z_, :, at : at + wide].astype(F32)
            return carry

        lax.fori_loop(0, PLANES, one, 0)
        tiles[s, :, :, :, at : at + wide] = flip[:, :, at : at + wide].reshape(2, 8, PLANES, wide).astype(BF16)

    def send_inside(v):
        s, lanes = MOVES[v][0], pl.ds(MOVES[v][1], MOVES[v][2])
        for g in range(2) if s == 0 else ((s - 1) // 2,):
            at = 0 if s == 0 else pl.ds(1 + 2 * ((s - 1) % 2), 2)
            n = 0 if s == 0 else 3 if v == 5 else 1 + (s - 1) % 2
            to_left, to_right = left.at[at, t, y, :, lanes], right.at[at, m, y, :, lanes]
            kk = g if s == 0 else pl.ds(0, 2)

            def from_left(h_, kk=kk):
                return tiles.at[s, kk, h_, :, lanes]

            def from_right(h_, kk=kk):
                return tiles.at[s, kk, 4 + h_, :, lanes]

            def to_owners(d, e, g=g, n=n, to_left=to_left, to_right=to_right, from_left=from_left, from_right=from_right):
                there = lax.rem(h + d, 4)
                pltpu.make_async_remote_copy(
                    src_ref=from_left(there), dst_ref=to_left, send_sem=pls.at[v], recv_sem=plr.at[n],
                    device_id=owner(g, there, a, lax.rem(b + e, 2)), device_id_type=MESH,
                ).start()
                pltpu.make_async_remote_copy(
                    src_ref=from_right(there), dst_ref=to_right, send_sem=prs.at[v], recv_sem=prr.at[n],
                    device_id=owner(g, there, lax.rem(a + e, 2), b), device_id_type=MESH,
                ).start()

            for e in range(2):

                def one(d, carry, e=e, to_owners=to_owners):
                    to_owners(d, e)
                    return carry

                lax.fori_loop(1 - e, 4, one, 0)

            @pl.when(core == g)
            def _(n=n, to_left=to_left, to_right=to_right, from_left=from_left, from_right=from_right):
                pltpu.make_async_copy(from_left(h), to_left, plr.at[n]).start()
                pltpu.make_async_copy(from_right(h), to_right, prr.at[n]).start()

            @pl.when(core != g)
            def _(to_owners=to_owners):
                to_owners(0, 0)

    def expect(n, at, lanes):
        for buffer, sem in ((left, plr), (right, prr)):
            arrived = buffer.at[at, :, :, :, lanes]
            pltpu.make_async_copy(arrived, arrived, sem.at[n]).wait()

    def multiply(chunks, columns, first=False):
        def unfold_block(i, carry):
            lanes = pl.ds(pl.multiple_of(i * 128, 128), 128)
            for n, (chunk, y_) in enumerate((chunk, y_) for chunk in chunks for y_ in range(2)):
                high = len(columns) * PLANES
                for source, target in ((left, lk), (right, rk)):
                    x = source[chunk, i, y_, :, : CUT if max(columns) < 4 else WIDE].astype(F32)
                    cols = [unfold(x, k) for k in columns]
                    target[n * high : n * high + high, lanes] = jnp.concatenate(cols, axis=0).astype(BF16)
            return carry

        lax.fori_loop(0, 8, unfold_block, 0)
        part = tn(rk[...], lk[...]).reshape(8, 128, 1024)[:, :ROWS]
        acc[...] = part if first else acc[...] + part

    def multiply_pair(n, split=False):
        pair = pl.ds(2 * n - 1, 2)
        expect(n, pair, pl.ds(0, CUT if split else WIDE))
        multiply((2 * n - 1, 2 * n), range(4))
        if split:
            expect(3, pair, pl.ds(CUT, REST))
        multiply((2 * n - 1, 2 * n), range(4, 8))

    def send_back(g):
        def to(d, part, start):
            t_, y_ = lax.rem(t + d // 2, 8), lax.rem(y + lax.rem(d, 2), 2)
            i = y_ * 8 + t_
            lanes = pl.ds(part * BACK[0], BACK[part])
            here, there = osend.at[i, :, lanes], oback.at[g, h, b, :, lanes]
            if start == 0:
                pltpu.make_async_copy(here, there, or_.at[2 * g + part]).start()
            else:
                pltpu.make_async_remote_copy(
                    src_ref=here, dst_ref=there, send_sem=os_.at[part], recv_sem=or_.at[2 * g + part],
                    device_id=(a * 8 + t_, z * 2 + y_), device_id_type=MESH,
                ).start()

        def block(d, start):
            t_, y_ = lax.rem(t + d // 2, 8), lax.rem(y + lax.rem(d, 2), 2)
            i = y_ * 8 + t_
            lanes = pl.ds(pl.multiple_of(t_ * 128, 128), 128)

            def pieces(q):
                rows = acc[:, pl.ds(pl.multiple_of(q * 16 + y_ * 8, 8), 8), lanes]
                turned = jnp.swapaxes(rows, 0, 1)
                return [turned[k] for k in range(STEP)]

            for qp in range(2):
                both = jnp.concatenate([fold(pieces(2 * qp + f), 0, 5) for f in range(2)], axis=0).astype(BF16)
                osend[i, :, qp * CUT : qp * CUT + CUT] = both[:, :CUT]
                osend[i, :, 2 * CUT + qp * REST : 2 * CUT + qp * REST + REST] = both[:, CUT:]
            last = pieces(4)
            both = jnp.concatenate([fold(last[:4], 0, 3), fold(last[4:], 0, 3)], axis=0).astype(BF16)
            osend[i, :, 2 * CUT + 2 * REST :] = both
            to(d, 0, start)

        def one(d, carry):
            block(d, 1)
            return carry

        def rest(d, carry):
            to(d, 1, 1)
            return carry

        lax.fori_loop(1, 16, one, 0)
        block(0, 0)
        lax.fori_loop(1, 16, rest, 0)
        to(0, 1, 0)

    def plane_of(b_, m_):
        return (m_ // 4) * 8 + b_ * 4 + m_ % 4

    def turn_back(g, part):
        arrived = oback.at[g, :, :, :, pl.ds(part * BACK[0], BACK[part])]
        pltpu.make_async_copy(arrived, arrived, or_.at[2 * g + part]).wait()
        at, wide = ((0, CUT), (CUT, REST))[part]
        lanes = slice(at, at + wide)

        def one(h_, carry):
            for b_ in range(2):
                for q in range(4):
                    begin = part * 2 * CUT + (q // 2) * wide
                    x = oback[g, h_, b_, :, begin : begin + wide].astype(F32)
                    flip[b_ * 8 : b_ * 8 + 8, q * 4 + h_, lanes] = x[(q % 2) * 8 : (q % 2) * 8 + 8]
            return carry

        lax.fori_loop(0, 4, one, 0)
        for b_ in range(2):
            for m_ in range(8):
                fsend[g, plane_of(b_, m_), :, lanes] = flip[b_ * 8 + m_, :, lanes].astype(BF16)

    def turn_back4():
        def one(i, carry):
            g, h_ = i // 4, lax.rem(i, 4)
            for b_ in range(2):
                x = oback[g, h_, b_, :, 2 * CUT + 2 * REST :].astype(F32)
                for f in range(2):
                    flip4[b_ * 8 : b_ * 8 + 8, f * 8 + i, :] = x[f * 8 : f * 8 + 8]
            return carry

        lax.fori_loop(0, 8, one, 0)
        for b_ in range(2):
            for m_ in range(8):
                fsend4[plane_of(b_, m_)] = flip4[b_ * 8 + m_].astype(BF16)

    def final(v, plane_out, plane_in):
        if v == 4:
            return fsend4.at[plane_out], fgot4.at[plane_in]
        lanes = pl.ds((v % 2) * CUT, (CUT, REST)[v % 2])
        return fsend.at[v // 2, plane_out, :, lanes], fgot.at[v // 2, plane_in, :, lanes]

    def send_final(v):
        here, to = final(v, z, z)
        pltpu.make_async_copy(here, to, fr.at[v]).start()

        def one(d, carry):
            there = lax.rem(z + d, PLANES)
            pltpu.make_async_remote_copy(
                src_ref=final(v, there, z)[0], dst_ref=to, send_sem=fs.at[v], recv_sem=fr.at[v],
                device_id=at_plane(there), device_id_type=MESH,
            ).start()
            return carry

        lax.fori_loop(1, PLANES, one, 0)

    def wait_final(v, sem, planes):
        target = final(v, z, pl.ds(0, planes))[1]
        pltpu.make_async_copy(target, target, sem.at[v]).wait()

    def project(x):
        centered = x - jnp.mean(x, axis=0, keepdims=True)
        variance = jnp.mean(centered * centered, axis=0, keepdims=True)
        return tn((centered * lax.rsqrt(variance + EPS)).astype(BF16), weights[5])

    def finish(qp):
        if qp < 2:
            rows = slice(qp * 8, qp * 8 + 8)
            both = mix_halves(fgot[0, :, rows, :].astype(F32), fgot[1, :, rows, :].astype(F32))
            for f in range(2):
                part = project(both[f].reshape(CH, WIDE))
                lin[f] = (part * gate[2 * qp + f]).reshape(STEP, ROWS, CH)
        else:
            x = fgot4[...].astype(F32)
            for f in range(2):
                part = project(x[:, f * 8 : f * 8 + 8, :].reshape(CH, SHORT_PAD))[:SHORT]
                lin[0, f * 4 : f * 4 + 4] = (part * gate[4, f * SHORT : f * SHORT + SHORT]).reshape(4, ROWS, CH)

        def eight_rows(n, carry):
            at = pl.multiple_of(lax.rem(n, 5) * 16 + (n // 5) * 8, 8)
            rows = pl.ds(pl.multiple_of(n * 8, 8), 8)
            if qp < 2:
                both = [jnp.swapaxes(lin[f, :, pl.ds(at, 8), :], 0, 1) for f in range(2)]
                out_ref[rows, qp * 16 : qp * 16 + 16, :] = jnp.concatenate(both, axis=1).astype(BF16)
            else:
                out_ref[rows, 32:40, :] = jnp.swapaxes(lin[0, :, pl.ds(at, 8), :], 0, 1).astype(BF16)
            return carry

        lax.fori_loop(0, 10, eight_rows, 0)

    normalise(4)
    lax.fori_loop(0, 4, single, 0)
    pl.semaphore_wait(barrier, 38)
    send_planes(0)
    for p in range(2):
        normalise(2 * p)
        normalise(2 * p + 1)
        double(p)
        send_planes(1 + p)
    for v in range(3, 6):
        send_planes(v)

    def gates(s, carry):
        gate[s] = jax.nn.sigmoid(jnp.dot(normed[s], weights[4], preferred_element_type=F32))
        return carry

    lax.fori_loop(0, CHUNKS, gates, 0)

    for v in range(4):
        arrive(v)
        turn(v)
        send_inside(v)
        if v == 1:
            expect(0, 0, pl.ds(0, WIDE))
            multiply((0,), range(8), True)
        if v >= 2:

            @pl.when(core == 0)
            def _(v=v):
                multiply_pair(v - 1)
                if v == 3:
                    send_back(0)

    arrive(4)
    turn(4)
    send_inside(4)

    @pl.when(core == 1)
    def _():
        multiply_pair(1)

    arrive(5)
    turn(5)
    send_inside(5)
    for part in range(2):
        turn_back(0, part)
        send_final(part)

    @pl.when(core == 1)
    def _():
        multiply_pair(2, True)
        send_back(1)

    for part in range(2):
        turn_back(1, part)
        send_final(2 + part)
    turn_back4()
    send_final(4)
    for v in range(4):
        wait_final(v, fr, PLANES)
    finish(0)
    finish(1)
    wait_final(4, fr, PLANES)
    finish(2)

    for v in range(6):
        s, lanes = MOVES[v][0], pl.ds(MOVES[v][1], MOVES[v][2])
        sent = got.at[s, pl.ds(0, PLANES - 1), :, lanes]
        pltpu.make_async_copy(sent, sent, zs.at[v]).wait()
        for here in range(2):
            n = 15 if v == 0 else 14 if here else 16
            sent = got.at[s, pl.ds(0, n), :, lanes]

            def inside(v=v, sent=sent):
                pltpu.make_async_copy(sent, sent, pls.at[v]).wait()
                pltpu.make_async_copy(sent, sent, prs.at[v]).wait()

            if v == 0 and here:
                inside()
            elif v:
                pl.when((core == (s - 1) // 2) == (here == 1))(inside)

    for part in range(2):
        sent = osend.at[pl.ds(0, 15), :, pl.ds(part * BACK[0], BACK[part])]
        pltpu.make_async_copy(sent, sent, os_.at[part]).wait()
    for v in range(5):
        wait_final(v, fs, PLANES - 1)


def on_device(*args):
    vmem, dma = pltpu.VMEM, pltpu.SemaphoreType.DMA
    return pl.pallas_call(
        kernel,
        out_shape=jax.ShapeDtypeStruct((ROWS, COLS, CH), BF16),
        in_specs=[pl.BlockSpec(memory_space=pl.ANY)] * 7,
        out_specs=pl.BlockSpec(memory_space=vmem),
        scratch_shapes=[
            vmem((ROWS, COLS, CH), BF16),
            vmem((6, CH, CH), BF16),
            vmem((ROWS, COLS, CH), F32),
            vmem((2, 256, CH), BF16),
            vmem((STEP, ROWS, CH), F32),
            vmem((CHUNKS, WIDE, CH), BF16),
            vmem((CHUNKS, WIDE, CH), F32),
            vmem((CHUNKS, PLANES, 16, WIDE), BF16),
            vmem((CHUNKS, PLANES, 16, WIDE), BF16),
            vmem((16, 16, WIDE), F32),
            vmem((CHUNKS, 2, 8, PLANES, WIDE), BF16),
            vmem((CHUNKS, 8, 2, PLANES, WIDE), BF16),
            vmem((CHUNKS, 8, 2, PLANES, WIDE), BF16),
            vmem((256, 1024), BF16),
            vmem((256, 1024), BF16),
            vmem((8, ROWS, 1024), F32),
            vmem((16, 16, sum(BACK)), BF16),
            vmem((2, 4, 2, 16, sum(BACK)), BF16),
            vmem((16, 16, SHORT_PAD), F32),
            vmem((2, PLANES, 16, WIDE), BF16),
            vmem((PLANES, 16, SHORT_PAD), BF16),
            vmem((2, PLANES, 16, WIDE), BF16),
            vmem((PLANES, 16, SHORT_PAD), BF16),
            vmem((2, STEP, ROWS, CH), F32),
            dma((7,)),
        ]
        + [dma((6,))] * 4
        + [dma((4,))] * 2
        + [dma((2,)), dma((4,)), dma((5,)), dma((5,))],
        compiler_params=pltpu.CompilerParams(collective_id=0, has_side_effects=True, vmem_limit_bytes=60 * 2**20),
        cost_estimate=pl.CostEstimate(flops=2_000_000_000, bytes_accessed=4_000_000, transcendentals=2_000_000),
    )(*args)


def solution(mesh):
    in_specs = (P("row", "chan", None), P(), P(), P(), P(), P(), P())
    return jax.shard_map(
        on_device, mesh=mesh, in_specs=in_specs, out_specs=P("row", "chan", None), check_vma=False
    )
```

```python
import functools

import jax
import jax.numpy as jnp
from jax import lax
from jax.experimental import pallas as pl
from jax.experimental.pallas import tpu as pltpu
from jax.sharding import PartitionSpec as P

MESH = pl.DeviceIdType.MESH
F32, BF16 = jnp.float32, jnp.bfloat16
EPS = 1e-05
ROWS, COLS, CH = 80, 40, 128
PLANES, CHUNKS, STEP = 16, 5, 8
WIDE = STEP * ROWS
SHORT, SHORT_PAD = WIDE // 2, 384
CUT, REST = 384, 256
EARLY, LATE, EARLY_COLS = 512, 128, 6
MOVES = [(0, 0, WIDE), (1, 0, WIDE), (2, 0, WIDE), (3, 0, WIDE), (4, 0, EARLY), (4, EARLY, LATE)]
BACK = (2 * CUT, 2 * REST + SHORT_PAD)


def nt(a, b):
    return lax.dot_general(a, b, (((1,), (1,)), ((), ())), preferred_element_type=F32)


def tn(a, b):
    return lax.dot_general(a, b, (((0,), (0,)), ((), ())), preferred_element_type=F32)


def unfold(x, k):
    start = k * ROWS
    tile, off = start // 128, start % 128
    lo = x[:, tile * 128 : tile * 128 + 128]
    if off == 0:
        return lo
    lo = pltpu.roll(lo, 128 - off, 1)
    if off + ROWS <= 128:
        return lo
    hi = pltpu.roll(x[:, tile * 128 + 128 : tile * 128 + 256], 128 - off, 1)
    lane = lax.broadcasted_iota(jnp.int32, lo.shape, 1)
    return jnp.where(lane < 128 - off, lo, hi)


def fold(pieces, first, last):
    tiles = {}
    lane = lax.broadcasted_iota(jnp.int32, pieces[0].shape, 1)
    for k, piece in enumerate(pieces):
        tile, off = k * ROWS // 128, k * ROWS % 128
        turned = pltpu.roll(piece, off, 1) if off else piece
        tiles[tile] = jnp.where(lane < off, tiles[tile], turned) if tile in tiles else turned
        if off + ROWS > 128:
            tiles[tile + 1] = turned
    return jnp.concatenate([tiles[tile] for tile in range(first, last)], axis=1)


def mix_halves(first, second):
    low = lax.broadcasted_iota(jnp.int32, first.shape, 1) < 4
    return jnp.where(low, first, pltpu.roll(second, 4, 1)), jnp.where(low, pltpu.roll(first, 4, 1), second)


def kernel(
    pair_hbm, wlg_hbm, wl_hbm, wrg_hbm, wr_hbm, wog_hbm, wo_hbm, out_ref,
    pair_ref, weights, pair32, wt, ns, normed, gate, send, got, flip, tiles, left, right, lk, rk, acc,
    osend, oback, flip4, fsend, fsend4, fgot, fgot4, lin,
    ins, zs, zr, pls, prs, plr, prr, os_, or_, fs, fr,
):
    r, c = lax.axis_index("row"), lax.axis_index("chan")
    z, y = c // 2, lax.rem(c, 2)
    a, t, core = r // 8, lax.rem(r, 8), lax.rem(r, 2)
    b = lax.rem(r // 4 + a, 2)
    m = a * 4 + lax.rem(r, 4)
    h = lax.rem(r // 2, 2) * 2 + y

    def owner(g, h_, a_, b_):
        return ((2 * a_ + lax.rem(a_ + b_, 2)) * 4 + (h_ // 2) * 2 + g, z * 2 + lax.rem(h_, 2))

    def at_plane(z_):
        return (r, z_ * 2 + y)

    loads = [pltpu.make_async_copy(pair_hbm, pair_ref, ins.at[0])]
    for n, ref in enumerate((wlg_hbm, wl_hbm, wrg_hbm, wr_hbm, wog_hbm, wo_hbm)):
        loads.append(pltpu.make_async_copy(ref, weights.at[n], ins.at[n + 1]))
    for load in loads:
        load.start()

    barrier = pltpu.get_barrier_semaphore()

    def greet_plane(d, carry):
        pl.semaphore_signal(barrier, inc=1, device_id=at_plane(lax.rem(z + d, PLANES)), device_id_type=MESH)
        return carry

    def greet_side(d, carry):
        there = (a * 8 + lax.rem(t + d // 2, 8), z * 2 + lax.rem(y + lax.rem(d, 2), 2))
        pl.semaphore_signal(barrier, inc=1, device_id=there, device_id_type=MESH)
        return carry

    def greet_across(d, carry):
        there = ((2 * (1 - a) + lax.rem(1 - a + b, 2)) * 4 + d // 2, z * 2 + lax.rem(d, 2))
        pl.semaphore_signal(barrier, inc=1, device_id=there, device_id_type=MESH)
        return carry

    lax.fori_loop(1, PLANES, greet_plane, 0)
    lax.fori_loop(1, 16, greet_side, 0)
    lax.fori_loop(0, 8, greet_across, 0)

    for load in loads:
        load.wait()
    for n in range(2):
        lt = weights[n].astype(F32).T.reshape(PLANES, 8, CH)
        rt = weights[n + 2].astype(F32).T.reshape(PLANES, 8, CH)
        wt[n] = jnp.concatenate(mix_halves(lt, rt), axis=1).reshape(256, CH).astype(BF16)
    pair32[...] = pair_ref[...].astype(F32)

    def normalise(s):
        def eight_rows(g, carry):
            x = pair32[pl.ds(pl.multiple_of(g * 8, 8), 8), pl.ds(pl.multiple_of(s * STEP, STEP), STEP), :]
            centered = x - jnp.mean(x, axis=-1, keepdims=True)
            variance = jnp.mean(centered * centered, axis=-1, keepdims=True)
            at = pl.multiple_of(lax.rem(g, 5) * 16 + (g // 5) * 8, 8)
            ns[:, pl.ds(at, 8), :] = jnp.swapaxes(centered * lax.rsqrt(variance + EPS), 0, 1)
            return carry

        lax.fori_loop(0, 10, eight_rows, 0)
        normed[s] = ns[...].reshape(WIDE, CH).astype(BF16)

    def factors(s, w):
        n = normed[s]
        rows = pl.ds(pl.multiple_of(w * 64, 64), 64)
        return (jax.nn.sigmoid(nt(wt[0, rows, :], n)) * nt(wt[1, rows, :], n)).reshape(4, 16, WIDE)

    def send_planes(v):
        s, lanes = MOVES[v][0], pl.ds(MOVES[v][1], MOVES[v][2])
        to = got.at[s, z, :, lanes]
        pltpu.make_async_copy(send.at[s, z, :, lanes], to, zr.at[v]).start()

        def one(d, carry):
            there = lax.rem(z + d, PLANES)
            pltpu.make_async_remote_copy(
                src_ref=send.at[s, there, :, lanes], dst_ref=to, send_sem=zs.at[v], recv_sem=zr.at[v],
                device_id=at_plane(there), device_id_type=MESH,
            ).start()
            return carry

        lax.fori_loop(1, PLANES, one, 0)

    def single(w, carry):
        send[0, pl.ds(w * 4, 4)] = factors(4, w).astype(BF16)
        return carry

    def double(p):
        def one(w, carry):
            v, u = factors(2 * p, w), factors(2 * p + 1, w)
            send[1 + p, pl.ds(w * 4, 4)] = jnp.concatenate([v[:, :8], u[:, :8]], axis=1).astype(BF16)
            send[3 + p, pl.ds(w * 4, 4)] = jnp.concatenate([v[:, 8:], u[:, 8:]], axis=1).astype(BF16)
            return carry

        lax.fori_loop(0, 4, one, 0)

    def arrive(v):
        arrived = got.at[MOVES[v][0], :, :, pl.ds(MOVES[v][1], MOVES[v][2])]
        pltpu.make_async_copy(arrived, arrived, zr.at[v]).wait()

    def turn(v):
        s, at, wide = MOVES[v]

        def one(z_, carry):
            flip[:, z_, at : at + wide] = got[s, z_, :, at : at + wide].astype(F32)
            return carry

        if wide > LATE:
            lax.fori_loop(0, PLANES, one, 0)
        else:
            for z_ in range(PLANES):
                flip[:, z_, at : at + wide] = got[s, z_, :, at : at + wide].astype(F32)
        tiles[s, :, :, :, at : at + wide] = flip[:, :, at : at + wide].reshape(2, 8, PLANES, wide).astype(BF16)

    def send_inside(v):
        s, lanes = MOVES[v][0], pl.ds(MOVES[v][1], MOVES[v][2])
        for g in range(2) if s == 0 else ((s - 1) // 2,):
            at = 0 if s == 0 else pl.ds(1 + 2 * ((s - 1) % 2), 2)
            n = 0 if s == 0 else 3 if v == 5 else 1 + (s - 1) % 2
            to_left, to_right = left.at[at, t, y, :, lanes], right.at[at, m, y, :, lanes]
            kk = g if s == 0 else pl.ds(0, 2)

            def from_left(h_, kk=kk):
                return tiles.at[s, kk, h_, :, lanes]

            def from_right(h_, kk=kk):
                return tiles.at[s, kk, 4 + h_, :, lanes]

            def to_owners(d, e, g=g, n=n, to_left=to_left, to_right=to_right, from_left=from_left, from_right=from_right):
                there = lax.rem(h + d, 4)
                pltpu.make_async_remote_copy(
                    src_ref=from_left(there), dst_ref=to_left, send_sem=pls.at[v], recv_sem=plr.at[n],
                    device_id=owner(g, there, a, lax.rem(b + e, 2)), device_id_type=MESH,
                ).start()
                pltpu.make_async_remote_copy(
                    src_ref=from_right(there), dst_ref=to_right, send_sem=prs.at[v], recv_sem=prr.at[n],
                    device_id=owner(g, there, lax.rem(a + e, 2), b), device_id_type=MESH,
                ).start()

            for e in range(2):

                def one(d, carry, e=e, to_owners=to_owners):
                    to_owners(d, e)
                    return carry

                lax.fori_loop(1 - e, 4, one, 0)

            @pl.when(core == g)
            def _(n=n, to_left=to_left, to_right=to_right, from_left=from_left, from_right=from_right):
                pltpu.make_async_copy(from_left(h), to_left, plr.at[n]).start()
                pltpu.make_async_copy(from_right(h), to_right, prr.at[n]).start()

            @pl.when(core != g)
            def _(to_owners=to_owners):
                to_owners(0, 0)

    def expect(n, at, lanes):
        for buffer, sem in ((left, plr), (right, prr)):
            arrived = buffer.at[at, :, :, :, lanes]
            pltpu.make_async_copy(arrived, arrived, sem.at[n]).wait()

    def multiply(chunks, columns, first=False):
        def unfold_block(i, carry):
            lanes = pl.ds(pl.multiple_of(i * 128, 128), 128)
            for n, (chunk, y_) in enumerate((chunk, y_) for chunk in chunks for y_ in range(2)):
                high = len(columns) * PLANES
                for source, target in ((left, lk), (right, rk)):
                    x = source[chunk, i, y_, :, : EARLY if max(columns) < EARLY_COLS else WIDE].astype(F32)
                    cols = [unfold(x, k) for k in columns]
                    target[n * high : n * high + high, lanes] = jnp.concatenate(cols, axis=0).astype(BF16)
            return carry

        lax.fori_loop(0, 8, unfold_block, 0)
        deep = len(chunks) * 2 * len(columns) * PLANES
        part = tn(rk[:deep], lk[:deep]).reshape(8, 128, 1024)[:, :ROWS]
        acc[...] = part if first else acc[...] + part

    def multiply_pair(n):
        expect(n, pl.ds(2 * n - 1, 2), pl.ds(0, WIDE))
        multiply((2 * n - 1, 2 * n), range(4))
        multiply((2 * n - 1, 2 * n), range(4, STEP))

    def multiply_last():
        expect(2, pl.ds(3, 2), pl.ds(0, EARLY))
        multiply((3, 4), range(EARLY_COLS))
        expect(3, pl.ds(3, 2), pl.ds(EARLY, LATE))
        multiply((3, 4), range(EARLY_COLS, STEP))

    def send_back(g):
        def to(d, part, start):
            t_, y_ = lax.rem(t + d // 2, 8), lax.rem(y + lax.rem(d, 2), 2)
            i = y_ * 8 + t_
            lanes = pl.ds(part * BACK[0], BACK[part])
            here, there = osend.at[i, :, lanes], oback.at[g, h, b, :, lanes]
            if start == 0:
                pltpu.make_async_copy(here, there, or_.at[2 * g + part]).start()
            else:
                pltpu.make_async_remote_copy(
                    src_ref=here, dst_ref=there, send_sem=os_.at[part], recv_sem=or_.at[2 * g + part],
                    device_id=(a * 8 + t_, z * 2 + y_), device_id_type=MESH,
                ).start()

        def block(d, start):
            t_, y_ = lax.rem(t + d // 2, 8), lax.rem(y + lax.rem(d, 2), 2)
            i = y_ * 8 + t_
            lanes = pl.ds(pl.multiple_of(t_ * 128, 128), 128)

            def pieces(q):
                rows = acc[:, pl.ds(pl.multiple_of(q * 16 + y_ * 8, 8), 8), lanes]
                turned = jnp.swapaxes(rows, 0, 1)
                return [turned[k] for k in range(STEP)]

            for qp in range(2):
                both = jnp.concatenate([fold(pieces(2 * qp + f), 0, 5) for f in range(2)], axis=0).astype(BF16)
                osend[i, :, qp * CUT : qp * CUT + CUT] = both[:, :CUT]
                osend[i, :, 2 * CUT + qp * REST : 2 * CUT + qp * REST + REST] = both[:, CUT:]
            last = pieces(4)
            both = jnp.concatenate([fold(last[:4], 0, 3), fold(last[4:], 0, 3)], axis=0).astype(BF16)
            osend[i, :, 2 * CUT + 2 * REST :] = both
            to(d, 0, start)

        def one(d, carry):
            block(d, 1)
            return carry

        def rest(d, carry):
            to(d, 1, 1)
            return carry

        lax.fori_loop(1, 16, one, 0)
        block(0, 0)
        lax.fori_loop(1, 16, rest, 0)
        to(0, 1, 0)

    def plane_of(b_, m_):
        return (m_ // 4) * 8 + (b_ + m_ // 4) % 2 * 4 + m_ % 4

    def turn_back(g, part):
        arrived = oback.at[g, :, :, :, pl.ds(part * BACK[0], BACK[part])]
        pltpu.make_async_copy(arrived, arrived, or_.at[2 * g + part]).wait()
        at, wide = ((0, CUT), (CUT, REST))[part]
        lanes = slice(at, at + wide)

        def one(h_, carry):
            for b_ in range(2):
                for q in range(4):
                    begin = part * 2 * CUT + (q // 2) * wide
                    x = oback[g, h_, b_, :, begin : begin + wide].astype(F32)
                    flip[b_ * 8 : b_ * 8 + 8, q * 4 + h_, lanes] = x[(q % 2) * 8 : (q % 2) * 8 + 8]
            return carry

        lax.fori_loop(0, 4, one, 0)
        for b_ in range(2):
            for m_ in range(8):
                fsend[g, plane_of(b_, m_), :, lanes] = flip[b_ * 8 + m_, :, lanes].astype(BF16)

    def turn_back4():
        def one(i, carry):
            g, h_ = i // 4, lax.rem(i, 4)
            for b_ in range(2):
                x = oback[g, h_, b_, :, 2 * CUT + 2 * REST :].astype(F32)
                for f in range(2):
                    flip4[b_ * 8 : b_ * 8 + 8, f * 8 + i, :] = x[f * 8 : f * 8 + 8]
            return carry

        lax.fori_loop(0, 8, one, 0)
        for b_ in range(2):
            for m_ in range(8):
                fsend4[plane_of(b_, m_)] = flip4[b_ * 8 + m_].astype(BF16)

    def final(v, plane_out, plane_in):
        if v == 4:
            return fsend4.at[plane_out], fgot4.at[plane_in]
        lanes = pl.ds((v % 2) * CUT, (CUT, REST)[v % 2])
        return fsend.at[v // 2, plane_out, :, lanes], fgot.at[v // 2, plane_in, :, lanes]

    def send_final(v):
        here, to = final(v, z, z)
        pltpu.make_async_copy(here, to, fr.at[v]).start()

        def one(d, carry):
            there = lax.rem(z + d, PLANES)
            pltpu.make_async_remote_copy(
                src_ref=final(v, there, z)[0], dst_ref=to, send_sem=fs.at[v], recv_sem=fr.at[v],
                device_id=at_plane(there), device_id_type=MESH,
            ).start()
            return carry

        lax.fori_loop(1, PLANES, one, 0)

    def wait_final(v, sem, planes):
        target = final(v, z, pl.ds(0, planes))[1]
        pltpu.make_async_copy(target, target, sem.at[v]).wait()

    def project(x):
        centered = x - jnp.mean(x, axis=0, keepdims=True)
        variance = jnp.mean(centered * centered, axis=0, keepdims=True)
        return tn((centered * lax.rsqrt(variance + EPS)).astype(BF16), weights[5])

    def finish(qp):
        if qp < 2:
            rows = slice(qp * 8, qp * 8 + 8)
            both = mix_halves(fgot[0, :, rows, :].astype(F32), fgot[1, :, rows, :].astype(F32))
            for f in range(2):
                part = project(both[f].reshape(CH, WIDE))
                lin[f] = (part * gate[2 * qp + f]).reshape(STEP, ROWS, CH)
        else:
            x = fgot4[...].astype(F32)
            for f in range(2):
                part = project(x[:, f * 8 : f * 8 + 8, :].reshape(CH, SHORT_PAD))[:SHORT]
                lin[0, f * 4 : f * 4 + 4] = (part * gate[4, f * SHORT : f * SHORT + SHORT]).reshape(4, ROWS, CH)

        def eight_rows(n, carry):
            at = pl.multiple_of(lax.rem(n, 5) * 16 + (n // 5) * 8, 8)
            rows = pl.ds(pl.multiple_of(n * 8, 8), 8)
            if qp < 2:
                both = [jnp.swapaxes(lin[f, :, pl.ds(at, 8), :], 0, 1) for f in range(2)]
                out_ref[rows, qp * 16 : qp * 16 + 16, :] = jnp.concatenate(both, axis=1).astype(BF16)
            else:
                out_ref[rows, 32:40, :] = jnp.swapaxes(lin[0, :, pl.ds(at, 8), :], 0, 1).astype(BF16)
            return carry

        lax.fori_loop(0, 10, eight_rows, 0)

    normalise(4)
    lax.fori_loop(0, 4, single, 0)
    pl.semaphore_wait(barrier, 38)
    send_planes(0)
    for p in range(2):
        normalise(2 * p)
        normalise(2 * p + 1)
        double(p)
        send_planes(1 + p)
    for v in range(3, 6):
        send_planes(v)

    def gates(s, carry):
        gate[s] = jax.nn.sigmoid(jnp.dot(normed[s], weights[4], preferred_element_type=F32))
        return carry

    lax.fori_loop(0, CHUNKS, gates, 0)

    for v in range(4):
        arrive(v)
        turn(v)
        send_inside(v)
        if v == 1:
            expect(0, 0, pl.ds(0, WIDE))
            multiply((0,), range(8), True)
        if v >= 2:

            @pl.when(core == 0)
            def _(v=v):
                multiply_pair(v - 1)
                if v == 3:
                    send_back(0)

    arrive(4)
    turn(4)
    send_inside(4)

    @pl.when(core == 1)
    def _():
        multiply_pair(1)

    arrive(5)
    turn(5)
    send_inside(5)
    for part in range(2):
        turn_back(0, part)
        send_final(part)

    @pl.when(core == 1)
    def _():
        multiply_last()
        send_back(1)

    for part in range(2):
        turn_back(1, part)
        send_final(2 + part)
    turn_back4()
    send_final(4)
    for v in range(4):
        wait_final(v, fr, PLANES)
    finish(0)
    finish(1)
    wait_final(4, fr, PLANES)
    finish(2)

    for v in range(6):
        s, lanes = MOVES[v][0], pl.ds(MOVES[v][1], MOVES[v][2])
        sent = got.at[s, pl.ds(0, PLANES - 1), :, lanes]
        pltpu.make_async_copy(sent, sent, zs.at[v]).wait()
        for here in range(2):
            n = 15 if v == 0 else 14 if here else 16
            sent = got.at[s, pl.ds(0, n), :, lanes]

            def inside(v=v, sent=sent):
                pltpu.make_async_copy(sent, sent, pls.at[v]).wait()
                pltpu.make_async_copy(sent, sent, prs.at[v]).wait()

            if v == 0 and here:
                inside()
            elif v:
                pl.when((core == (s - 1) // 2) == (here == 1))(inside)

    for part in range(2):
        sent = osend.at[pl.ds(0, 15), :, pl.ds(part * BACK[0], BACK[part])]
        pltpu.make_async_copy(sent, sent, os_.at[part]).wait()
    for v in range(5):
        wait_final(v, fs, PLANES - 1)


def on_device(*args):
    vmem, dma = pltpu.VMEM, pltpu.SemaphoreType.DMA
    return pl.pallas_call(
        kernel,
        out_shape=jax.ShapeDtypeStruct((ROWS, COLS, CH), BF16),
        in_specs=[pl.BlockSpec(memory_space=pl.ANY)] * 7,
        out_specs=pl.BlockSpec(memory_space=vmem),
        scratch_shapes=[
            vmem((ROWS, COLS, CH), BF16),
            vmem((6, CH, CH), BF16),
            vmem((ROWS, COLS, CH), F32),
            vmem((2, 256, CH), BF16),
            vmem((STEP, ROWS, CH), F32),
            vmem((CHUNKS, WIDE, CH), BF16),
            vmem((CHUNKS, WIDE, CH), F32),
            vmem((CHUNKS, PLANES, 16, WIDE), BF16),
            vmem((CHUNKS, PLANES, 16, WIDE), BF16),
            vmem((16, 16, WIDE), F32),
            vmem((CHUNKS, 2, 8, PLANES, WIDE), BF16),
            vmem((CHUNKS, 8, 2, PLANES, WIDE), BF16),
            vmem((CHUNKS, 8, 2, PLANES, WIDE), BF16),
            vmem((384, 1024), BF16),
            vmem((384, 1024), BF16),
            vmem((8, ROWS, 1024), F32),
            vmem((16, 16, sum(BACK)), BF16),
            vmem((2, 4, 2, 16, sum(BACK)), BF16),
            vmem((16, 16, SHORT_PAD), F32),
            vmem((2, PLANES, 16, WIDE), BF16),
            vmem((PLANES, 16, SHORT_PAD), BF16),
            vmem((2, PLANES, 16, WIDE), BF16),
            vmem((PLANES, 16, SHORT_PAD), BF16),
            vmem((2, STEP, ROWS, CH), F32),
            dma((7,)),
        ]
        + [dma((6,))] * 4
        + [dma((4,))] * 2
        + [dma((2,)), dma((4,)), dma((5,)), dma((5,))],
        compiler_params=pltpu.CompilerParams(collective_id=0, has_side_effects=True, vmem_limit_bytes=60 * 2**20),
        cost_estimate=pl.CostEstimate(flops=2_000_000_000, bytes_accessed=4_000_000, transcendentals=2_000_000),
    )(*args)


def solution(mesh):
    in_specs = (P("row", "chan", None), P(), P(), P(), P(), P(), P())
    return jax.shard_map(
        on_device, mesh=mesh, in_specs=in_specs, out_specs=P("row", "chan", None), check_vma=False
    )
```

```python
import functools

import jax
import jax.numpy as jnp
from jax import lax
from jax.experimental import pallas as pl
from jax.experimental.pallas import tpu as pltpu
from jax.sharding import PartitionSpec as P

MESH = pl.DeviceIdType.MESH
F32, BF16 = jnp.float32, jnp.bfloat16
EPS = 1e-05
ROWS, COLS, CH = 80, 40, 128
PLANES, CHUNKS, STEP = 16, 5, 8
WIDE = STEP * ROWS
SHORT, SHORT_PAD = WIDE // 2, 384
CUT, REST = 256, 384
EARLY, LATE, EARLY_COLS = 512, 128, 6
MOVES = [(0, 0, WIDE), (1, 0, WIDE), (2, 0, WIDE), (3, 0, WIDE), (4, 0, EARLY), (4, EARLY, LATE)]
BACK = (2 * CUT, 2 * REST + SHORT_PAD)


def nt(a, b):
    return lax.dot_general(a, b, (((1,), (1,)), ((), ())), preferred_element_type=F32)


def tn(a, b):
    return lax.dot_general(a, b, (((0,), (0,)), ((), ())), preferred_element_type=F32)


def unfold(x, k):
    start = k * ROWS
    tile, off = start // 128, start % 128
    lo = x[:, tile * 128 : tile * 128 + 128]
    if off == 0:
        return lo
    lo = pltpu.roll(lo, 128 - off, 1)
    if off + ROWS <= 128:
        return lo
    hi = pltpu.roll(x[:, tile * 128 + 128 : tile * 128 + 256], 128 - off, 1)
    lane = lax.broadcasted_iota(jnp.int32, lo.shape, 1)
    return jnp.where(lane < 128 - off, lo, hi)


def fold(pieces, first, last):
    tiles = {}
    lane = lax.broadcasted_iota(jnp.int32, pieces[0].shape, 1)
    for k, piece in enumerate(pieces):
        tile, off = k * ROWS // 128, k * ROWS % 128
        turned = pltpu.roll(piece, off, 1) if off else piece
        tiles[tile] = jnp.where(lane < off, tiles[tile], turned) if tile in tiles else turned
        if off + ROWS > 128:
            tiles[tile + 1] = turned
    return jnp.concatenate([tiles[tile] for tile in range(first, last)], axis=1)


def mix_halves(first, second):
    low = lax.broadcasted_iota(jnp.int32, first.shape, 1) < 4
    return jnp.where(low, first, pltpu.roll(second, 4, 1)), jnp.where(low, pltpu.roll(first, 4, 1), second)


def kernel(
    pair_hbm, wlg_hbm, wl_hbm, wrg_hbm, wr_hbm, wog_hbm, wo_hbm, out_ref,
    pair_ref, weights, pair32, wt, ns, normed, gate, send, got, flip, tiles, left, right, lk, rk, acc,
    osend, oback, flip4, fsend, fsend4, fgot, fgot4, lin,
    ins, zs, zr, pls, prs, plr, prr, os_, or_, fs, fr,
):
    r, c = lax.axis_index("row"), lax.axis_index("chan")
    z, y = c // 2, lax.rem(c, 2)
    a, t, core = r // 8, lax.rem(r, 8), lax.rem(r, 2)
    b = lax.rem(r // 4 + a, 2)
    m = a * 4 + lax.rem(r, 4)
    h = lax.rem(r // 2, 2) * 2 + y

    def owner(g, h_, a_, b_):
        return ((2 * a_ + lax.rem(a_ + b_, 2)) * 4 + (h_ // 2) * 2 + g, z * 2 + lax.rem(h_, 2))

    def at_plane(z_):
        return (r, z_ * 2 + y)

    loads = [pltpu.make_async_copy(pair_hbm, pair_ref, ins.at[0])]
    for n, ref in enumerate((wlg_hbm, wl_hbm, wrg_hbm, wr_hbm, wog_hbm, wo_hbm)):
        loads.append(pltpu.make_async_copy(ref, weights.at[n], ins.at[n + 1]))
    for load in loads:
        load.start()

    barrier = pltpu.get_barrier_semaphore()

    def greet_plane(d, carry):
        pl.semaphore_signal(barrier, inc=1, device_id=at_plane(lax.rem(z + d, PLANES)), device_id_type=MESH)
        return carry

    def greet_side(d, carry):
        there = (a * 8 + lax.rem(t + d // 2, 8), z * 2 + lax.rem(y + lax.rem(d, 2), 2))
        pl.semaphore_signal(barrier, inc=1, device_id=there, device_id_type=MESH)
        return carry

    def greet_across(d, carry):
        there = ((2 * (1 - a) + lax.rem(1 - a + b, 2)) * 4 + d // 2, z * 2 + lax.rem(d, 2))
        pl.semaphore_signal(barrier, inc=1, device_id=there, device_id_type=MESH)
        return carry

    lax.fori_loop(1, PLANES, greet_plane, 0)
    lax.fori_loop(1, 16, greet_side, 0)
    lax.fori_loop(0, 8, greet_across, 0)

    for load in loads:
        load.wait()
    for n in range(2):
        lt = weights[n].astype(F32).T.reshape(PLANES, 8, CH)
        rt = weights[n + 2].astype(F32).T.reshape(PLANES, 8, CH)
        wt[n] = jnp.concatenate(mix_halves(lt, rt), axis=1).reshape(256, CH).astype(BF16)
    pair32[...] = pair_ref[...].astype(F32)

    def normalise(s):
        def eight_rows(g, carry):
            x = pair32[pl.ds(pl.multiple_of(g * 8, 8), 8), pl.ds(pl.multiple_of(s * STEP, STEP), STEP), :]
            centered = x - jnp.mean(x, axis=-1, keepdims=True)
            variance = jnp.mean(centered * centered, axis=-1, keepdims=True)
            at = pl.multiple_of(lax.rem(g, 5) * 16 + (g // 5) * 8, 8)
            ns[:, pl.ds(at, 8), :] = jnp.swapaxes(centered * lax.rsqrt(variance + EPS), 0, 1)
            return carry

        lax.fori_loop(0, 10, eight_rows, 0)
        normed[s] = ns[...].reshape(WIDE, CH).astype(BF16)

    def factors(s, w):
        n = normed[s]
        rows = pl.ds(pl.multiple_of(w * 64, 64), 64)
        return (jax.nn.sigmoid(nt(wt[0, rows, :], n)) * nt(wt[1, rows, :], n)).reshape(4, 16, WIDE)

    def send_planes(v):
        s, lanes = MOVES[v][0], pl.ds(MOVES[v][1], MOVES[v][2])
        to = got.at[s, z, :, lanes]
        pltpu.make_async_copy(send.at[s, z, :, lanes], to, zr.at[v]).start()

        def one(d, carry):
            there = lax.rem(z + d, PLANES)
            pltpu.make_async_remote_copy(
                src_ref=send.at[s, there, :, lanes], dst_ref=to, send_sem=zs.at[v], recv_sem=zr.at[v],
                device_id=at_plane(there), device_id_type=MESH,
            ).start()
            return carry

        lax.fori_loop(1, PLANES, one, 0)

    def single(w, carry):
        send[0, pl.ds(w * 4, 4)] = factors(4, w).astype(BF16)
        return carry

    def double(p):
        def one(w, carry):
            v, u = factors(2 * p, w), factors(2 * p + 1, w)
            send[1 + p, pl.ds(w * 4, 4)] = jnp.concatenate([v[:, :8], u[:, :8]], axis=1).astype(BF16)
            send[3 + p, pl.ds(w * 4, 4)] = jnp.concatenate([v[:, 8:], u[:, 8:]], axis=1).astype(BF16)
            return carry

        lax.fori_loop(0, 4, one, 0)

    def arrive(v):
        arrived = got.at[MOVES[v][0], :, :, pl.ds(MOVES[v][1], MOVES[v][2])]
        pltpu.make_async_copy(arrived, arrived, zr.at[v]).wait()

    def turn(v):
        s, at, wide = MOVES[v]

        def one(z_, carry):
            flip[:, z_, at : at + wide] = got[s, z_, :, at : at + wide].astype(F32)
            return carry

        if wide > LATE:
            lax.fori_loop(0, PLANES, one, 0)
        else:
            for z_ in range(PLANES):
                flip[:, z_, at : at + wide] = got[s, z_, :, at : at + wide].astype(F32)
        tiles[s, :, :, :, at : at + wide] = flip[:, :, at : at + wide].reshape(2, 8, PLANES, wide).astype(BF16)

    def send_inside(v):
        s, lanes = MOVES[v][0], pl.ds(MOVES[v][1], MOVES[v][2])
        for g in range(2) if s == 0 else ((s - 1) // 2,):
            at = 0 if s == 0 else pl.ds(1 + 2 * ((s - 1) % 2), 2)
            n = 0 if s == 0 else 3 if v == 5 else 1 + (s - 1) % 2
            to_left, to_right = left.at[at, t, y, :, lanes], right.at[at, m, y, :, lanes]
            kk = g if s == 0 else pl.ds(0, 2)

            def from_left(h_, kk=kk):
                return tiles.at[s, kk, h_, :, lanes]

            def from_right(h_, kk=kk):
                return tiles.at[s, kk, 4 + h_, :, lanes]

            def to_owners(d, e, g=g, n=n, to_left=to_left, to_right=to_right, from_left=from_left, from_right=from_right):
                there = lax.rem(h + d, 4)
                pltpu.make_async_remote_copy(
                    src_ref=from_left(there), dst_ref=to_left, send_sem=pls.at[v], recv_sem=plr.at[n],
                    device_id=owner(g, there, a, lax.rem(b + e, 2)), device_id_type=MESH,
                ).start()
                pltpu.make_async_remote_copy(
                    src_ref=from_right(there), dst_ref=to_right, send_sem=prs.at[v], recv_sem=prr.at[n],
                    device_id=owner(g, there, lax.rem(a + e, 2), b), device_id_type=MESH,
                ).start()

            for e in range(2):

                def one(d, carry, e=e, to_owners=to_owners):
                    to_owners(d, e)
                    return carry

                lax.fori_loop(1 - e, 4, one, 0)

            @pl.when(core == g)
            def _(n=n, to_left=to_left, to_right=to_right, from_left=from_left, from_right=from_right):
                pltpu.make_async_copy(from_left(h), to_left, plr.at[n]).start()
                pltpu.make_async_copy(from_right(h), to_right, prr.at[n]).start()

            @pl.when(core != g)
            def _(to_owners=to_owners):
                to_owners(0, 0)

    def expect(n, at, lanes):
        for buffer, sem in ((left, plr), (right, prr)):
            arrived = buffer.at[at, :, :, :, lanes]
            pltpu.make_async_copy(arrived, arrived, sem.at[n]).wait()

    def multiply(chunks, columns, first=False):
        def unfold_block(i, carry):
            lanes = pl.ds(pl.multiple_of(i * 128, 128), 128)
            for n, (chunk, y_) in enumerate((chunk, y_) for chunk in chunks for y_ in range(2)):
                high = len(columns) * PLANES
                for source, target in ((left, lk), (right, rk)):
                    x = source[chunk, i, y_, :, : EARLY if max(columns) < EARLY_COLS else WIDE].astype(F32)
                    cols = [unfold(x, k) for k in columns]
                    target[n * high : n * high + high, lanes] = jnp.concatenate(cols, axis=0).astype(BF16)
            return carry

        lax.fori_loop(0, 8, unfold_block, 0)
        deep = len(chunks) * 2 * len(columns) * PLANES
        part = tn(rk[:deep], lk[:deep]).reshape(8, 128, 1024)[:, :ROWS]
        acc[...] = part if first else acc[...] + part

    def multiply_pair(n):
        expect(n, pl.ds(2 * n - 1, 2), pl.ds(0, WIDE))
        multiply((2 * n - 1, 2 * n), range(4))
        multiply((2 * n - 1, 2 * n), range(4, STEP))

    def multiply_last():
        expect(2, pl.ds(3, 2), pl.ds(0, EARLY))
        multiply((3, 4), range(EARLY_COLS))
        expect(3, pl.ds(3, 2), pl.ds(EARLY, LATE))
        multiply((3, 4), range(EARLY_COLS, STEP))

    def send_back(g):
        def to(d, part, start):
            t_, y_ = lax.rem(t + d // 2, 8), lax.rem(y + lax.rem(d, 2), 2)
            i = y_ * 8 + t_
            lanes = pl.ds(part * BACK[0], BACK[part])
            here, there = osend.at[i, :, lanes], oback.at[g, h, b, :, lanes]
            if start == 0:
                pltpu.make_async_copy(here, there, or_.at[2 * g + part]).start()
            else:
                pltpu.make_async_remote_copy(
                    src_ref=here, dst_ref=there, send_sem=os_.at[part], recv_sem=or_.at[2 * g + part],
                    device_id=(a * 8 + t_, z * 2 + y_), device_id_type=MESH,
                ).start()

        def block(d, start):
            t_, y_ = lax.rem(t + d // 2, 8), lax.rem(y + lax.rem(d, 2), 2)
            i = y_ * 8 + t_
            lanes = pl.ds(pl.multiple_of(t_ * 128, 128), 128)

            def pieces(q):
                rows = acc[:, pl.ds(pl.multiple_of(q * 16 + y_ * 8, 8), 8), lanes]
                turned = jnp.swapaxes(rows, 0, 1)
                return [turned[k] for k in range(STEP)]

            for qp in range(2):
                both = jnp.concatenate([fold(pieces(2 * qp + f), 0, 5) for f in range(2)], axis=0).astype(BF16)
                osend[i, :, qp * CUT : qp * CUT + CUT] = both[:, :CUT]
                osend[i, :, 2 * CUT + qp * REST : 2 * CUT + qp * REST + REST] = both[:, CUT:]
            last = pieces(4)
            both = jnp.concatenate([fold(last[:4], 0, 3), fold(last[4:], 0, 3)], axis=0).astype(BF16)
            osend[i, :, 2 * CUT + 2 * REST :] = both
            to(d, 0, start)

        def one(d, carry):
            block(d, 1)
            return carry

        def rest(d, carry):
            to(d, 1, 1)
            return carry

        lax.fori_loop(1, 16, one, 0)
        block(0, 0)
        lax.fori_loop(1, 16, rest, 0)
        to(0, 1, 0)

    def plane_of(b_, m_):
        return (m_ // 4) * 8 + (b_ + m_ // 4) % 2 * 4 + m_ % 4

    def turn_back(g, part):
        arrived = oback.at[g, :, :, :, pl.ds(part * BACK[0], BACK[part])]
        pltpu.make_async_copy(arrived, arrived, or_.at[2 * g + part]).wait()
        at, wide = ((0, CUT), (CUT, REST))[part]
        lanes = slice(at, at + wide)

        def one(h_, carry):
            for b_ in range(2):
                for q in range(4):
                    begin = part * 2 * CUT + (q // 2) * wide
                    x = oback[g, h_, b_, :, begin : begin + wide].astype(F32)
                    flip[b_ * 8 : b_ * 8 + 8, q * 4 + h_, lanes] = x[(q % 2) * 8 : (q % 2) * 8 + 8]
            return carry

        lax.fori_loop(0, 4, one, 0)
        for b_ in range(2):
            for m_ in range(8):
                fsend[g, plane_of(b_, m_), :, lanes] = flip[b_ * 8 + m_, :, lanes].astype(BF16)

    def turn_back4():
        def one(i, carry):
            g, h_ = i // 4, lax.rem(i, 4)
            for b_ in range(2):
                x = oback[g, h_, b_, :, 2 * CUT + 2 * REST :].astype(F32)
                for f in range(2):
                    flip4[b_ * 8 : b_ * 8 + 8, f * 8 + i, :] = x[f * 8 : f * 8 + 8]
            return carry

        lax.fori_loop(0, 8, one, 0)
        for b_ in range(2):
            for m_ in range(8):
                fsend4[plane_of(b_, m_)] = flip4[b_ * 8 + m_].astype(BF16)

    def final(v, plane_out, plane_in):
        if v == 4:
            return fsend4.at[plane_out], fgot4.at[plane_in]
        lanes = pl.ds((v % 2) * CUT, (CUT, REST)[v % 2])
        return fsend.at[v // 2, plane_out, :, lanes], fgot.at[v // 2, plane_in, :, lanes]

    def send_final(v):
        here, to = final(v, z, z)
        pltpu.make_async_copy(here, to, fr.at[v]).start()

        def one(d, carry):
            there = lax.rem(z + d, PLANES)
            pltpu.make_async_remote_copy(
                src_ref=final(v, there, z)[0], dst_ref=to, send_sem=fs.at[v], recv_sem=fr.at[v],
                device_id=at_plane(there), device_id_type=MESH,
            ).start()
            return carry

        lax.fori_loop(1, PLANES, one, 0)

    def wait_final(v, sem, planes):
        target = final(v, z, pl.ds(0, planes))[1]
        pltpu.make_async_copy(target, target, sem.at[v]).wait()

    def project(x):
        centered = x - jnp.mean(x, axis=0, keepdims=True)
        variance = jnp.mean(centered * centered, axis=0, keepdims=True)
        return tn((centered * lax.rsqrt(variance + EPS)).astype(BF16), weights[5])

    def finish(qp):
        if qp < 2:
            rows = slice(qp * 8, qp * 8 + 8)
            both = mix_halves(fgot[0, :, rows, :].astype(F32), fgot[1, :, rows, :].astype(F32))
            for f in range(2):
                part = project(both[f].reshape(CH, WIDE))
                lin[f] = (part * gate[2 * qp + f]).reshape(STEP, ROWS, CH)
        else:
            x = fgot4[...].astype(F32)
            for f in range(2):
                part = project(x[:, f * 8 : f * 8 + 8, :].reshape(CH, SHORT_PAD))[:SHORT]
                lin[0, f * 4 : f * 4 + 4] = (part * gate[4, f * SHORT : f * SHORT + SHORT]).reshape(4, ROWS, CH)

        def eight_rows(n, carry):
            at = pl.multiple_of(lax.rem(n, 5) * 16 + (n // 5) * 8, 8)
            rows = pl.ds(pl.multiple_of(n * 8, 8), 8)
            if qp < 2:
                both = [jnp.swapaxes(lin[f, :, pl.ds(at, 8), :], 0, 1) for f in range(2)]
                out_ref[rows, qp * 16 : qp * 16 + 16, :] = jnp.concatenate(both, axis=1).astype(BF16)
            else:
                out_ref[rows, 32:40, :] = jnp.swapaxes(lin[0, :, pl.ds(at, 8), :], 0, 1).astype(BF16)
            return carry

        lax.fori_loop(0, 10, eight_rows, 0)

    normalise(4)
    lax.fori_loop(0, 4, single, 0)
    pl.semaphore_wait(barrier, 38)
    send_planes(0)
    for p in range(2):
        normalise(2 * p)
        normalise(2 * p + 1)
        double(p)
        send_planes(1 + p)
    for v in range(3, 6):
        send_planes(v)

    def gates(s, carry):
        gate[s] = jax.nn.sigmoid(jnp.dot(normed[s], weights[4], preferred_element_type=F32))
        return carry

    lax.fori_loop(0, CHUNKS, gates, 0)

    for v in range(4):
        arrive(v)
        turn(v)
        send_inside(v)
        if v == 1:
            expect(0, 0, pl.ds(0, WIDE))
            multiply((0,), range(8), True)
        if v >= 2:

            @pl.when(core == 0)
            def _(v=v):
                multiply_pair(v - 1)
                if v == 3:
                    send_back(0)

    arrive(4)
    turn(4)
    send_inside(4)

    @pl.when(core == 1)
    def _():
        multiply_pair(1)

    arrive(5)
    turn(5)
    send_inside(5)
    for part in range(2):
        turn_back(0, part)
        send_final(part)

    @pl.when(core == 1)
    def _():
        multiply_last()
        send_back(1)

    for part in range(2):
        turn_back(1, part)
        send_final(2 + part)
    turn_back4()
    send_final(4)
    for v in range(4):
        wait_final(v, fr, PLANES)
    finish(0)
    finish(1)
    wait_final(4, fr, PLANES)
    finish(2)

    for v in range(6):
        s, lanes = MOVES[v][0], pl.ds(MOVES[v][1], MOVES[v][2])
        sent = got.at[s, pl.ds(0, PLANES - 1), :, lanes]
        pltpu.make_async_copy(sent, sent, zs.at[v]).wait()
        for here in range(2):
            n = 15 if v == 0 else 14 if here else 16
            sent = got.at[s, pl.ds(0, n), :, lanes]

            def inside(v=v, sent=sent):
                pltpu.make_async_copy(sent, sent, pls.at[v]).wait()
                pltpu.make_async_copy(sent, sent, prs.at[v]).wait()

            if v == 0 and here:
                inside()
            elif v:
                pl.when((core == (s - 1) // 2) == (here == 1))(inside)

    for part in range(2):
        sent = osend.at[pl.ds(0, 15), :, pl.ds(part * BACK[0], BACK[part])]
        pltpu.make_async_copy(sent, sent, os_.at[part]).wait()
    for v in range(5):
        wait_final(v, fs, PLANES - 1)


def on_device(*args):
    vmem, dma = pltpu.VMEM, pltpu.SemaphoreType.DMA
    return pl.pallas_call(
        kernel,
        out_shape=jax.ShapeDtypeStruct((ROWS, COLS, CH), BF16),
        in_specs=[pl.BlockSpec(memory_space=pl.ANY)] * 7,
        out_specs=pl.BlockSpec(memory_space=vmem),
        scratch_shapes=[
            vmem((ROWS, COLS, CH), BF16),
            vmem((6, CH, CH), BF16),
            vmem((ROWS, COLS, CH), F32),
            vmem((2, 256, CH), BF16),
            vmem((STEP, ROWS, CH), F32),
            vmem((CHUNKS, WIDE, CH), BF16),
            vmem((CHUNKS, WIDE, CH), F32),
            vmem((CHUNKS, PLANES, 16, WIDE), BF16),
            vmem((CHUNKS, PLANES, 16, WIDE), BF16),
            vmem((16, 16, WIDE), F32),
            vmem((CHUNKS, 2, 8, PLANES, WIDE), BF16),
            vmem((CHUNKS, 8, 2, PLANES, WIDE), BF16),
            vmem((CHUNKS, 8, 2, PLANES, WIDE), BF16),
            vmem((384, 1024), BF16),
            vmem((384, 1024), BF16),
            vmem((8, ROWS, 1024), F32),
            vmem((16, 16, sum(BACK)), BF16),
            vmem((2, 4, 2, 16, sum(BACK)), BF16),
            vmem((16, 16, SHORT_PAD), F32),
            vmem((2, PLANES, 16, WIDE), BF16),
            vmem((PLANES, 16, SHORT_PAD), BF16),
            vmem((2, PLANES, 16, WIDE), BF16),
            vmem((PLANES, 16, SHORT_PAD), BF16),
            vmem((2, STEP, ROWS, CH), F32),
            dma((7,)),
        ]
        + [dma((6,))] * 4
        + [dma((4,))] * 2
        + [dma((2,)), dma((4,)), dma((5,)), dma((5,))],
        compiler_params=pltpu.CompilerParams(collective_id=0, has_side_effects=True, vmem_limit_bytes=60 * 2**20),
        cost_estimate=pl.CostEstimate(flops=2_000_000_000, bytes_accessed=4_000_000, transcendentals=2_000_000),
    )(*args)


def solution(mesh):
    in_specs = (P("row", "chan", None), P(), P(), P(), P(), P(), P())
    return jax.shard_map(
        on_device, mesh=mesh, in_specs=in_specs, out_specs=P("row", "chan", None), check_vma=False
    )
```
